512 devices in a mesh: gx: 64 (over y_lo, z, core), ha: 8 (over y_hi, x).
Axes of the slice: x: 4, y: 8 (y_hi: 2, y_lo: 4; y = y_hi * 4 + y_lo), z: 8, core: 2. Of those that a mesh axis runs over, the one named last changes fastest.
Arguments:
- wall_history: bfloat16 [3, 3, 8192, 1024], P(None, None, 'gx', 'ha'), may hold values from -6 to 6
- kernel_taps: bfloat16 [8, 3, 3, 257], P('ha'), may hold values from -0.125 to 0.125
- span_gains: float32 [8, 9], P('ha'), may hold values from -2 to 2
Outputs:
- velocity: float32 [8, 8192, 1024], P('ha', 'gx')
The draws below stay inside these ranges and needn't reach their ends.
All inputs are finite; a program needn't handle non-finite values.
Results may differ from the reference program's by a relative error of at most 0.0003.
Values may be sent and summed in bfloat16 or wider, within the bound.
No kernel may reach another device: no remote copies, remote signals or barrier semaphores. Data moves between devices by JAX's collectives and lax.ppermute only.
A program may use at most 64 MiB of HBM per device.

```python
import jax
import jax.numpy as jnp
from jax import lax

SNAP = 3
CHAN = 3
R = 128
SPAN = 9
TAPS = 257
NX = 8192
NZ = 1024
HEIGHTS = 8


def block_scale(key, shape, split, least, largest):
    factor_of = 1.0
    for dim, parts in split:
        steps = jax.random.uniform(jax.random.fold_in(jax.random.fold_in(key, 6), dim), (parts,), jnp.float32, least / len(split), largest / len(split))
        factor_of = factor_of * jnp.repeat(jnp.exp(steps), shape[dim] // parts).reshape((-1,) + (1,) * (len(shape) - 1 - dim))
    return factor_of


def gaussian(rng, extent, width, bound, cuts=(), held_as=jnp.bfloat16):
    level = block_scale(rng, extent, cuts, -0.22, 0.18) if cuts else 1.0
    values = jax.random.normal(rng, extent, jnp.float32) * width * level
    return jnp.minimum(jnp.maximum(values, -bound), bound).astype(held_as)


def setup_inputs(seed: int = 0) -> dict:
    key_of = jax.random.split(jax.random.key(seed), 4)
    wall_history = gaussian(key_of[0], (SNAP, CHAN, NX, NZ), 1.0, 6.0, ((2, 64), (3, 8)))
    kernel_taps = gaussian(key_of[1], (HEIGHTS, SNAP, CHAN, TAPS), (SNAP * CHAN * TAPS) ** -0.5, 0.125, ((0, 8),))
    span_gains = gaussian(key_of[2], (HEIGHTS, SPAN), SPAN ** -0.5, 2.0, ((0, 8),), jnp.float32)
    return {"wall_history": wall_history, "kernel_taps": kernel_taps, "span_gains": span_gains}


def reference(wall_history, kernel_taps, span_gains):
    data = wall_history.astype(jnp.float32).reshape(SNAP * CHAN, NX, NZ)
    padded = jnp.concatenate([data[:, NX - R:], data, data[:, :R]], axis=1)[None]
    kernels = kernel_taps.astype(jnp.float32).reshape(HEIGHTS, SNAP * CHAN, TAPS, 1)

    def one_height(pair):
        kernel, gains = pair
        read = lax.conv_general_dilated(padded, kernel[None], (1, 1), "VALID",
                                            dimension_numbers=("NCHW", "OIHW", "NCHW"),
                                            precision=lax.Precision.HIGHEST)[0, 0]
        half = (SPAN - 1) // 2
        result = jnp.zeros((NX, NZ), jnp.float32)
        for shift in range(SPAN):
            result = result + gains[shift] * jnp.roll(read, half - shift, axis=1)
        return result

    return lax.map(one_height, (kernels, span_gains))
```

```python
import jax
import jax.numpy as jnp
from jax import lax
from jax.experimental import pallas as pl
from jax.experimental.pallas import tpu as pltpu
from jax.sharding import PartitionSpec as P

SUB = 32


def band_kernel(parity_ref, rows_ref, own_ref, near_ref, far_ref, read_ref, band_ref):
    planes, cells, width = own_ref.shape
    heights = rows_ref.shape[0]
    depth = rows_ref.shape[1]
    window = 2 * cells + SUB
    for h in range(heights):
        row = jnp.broadcast_to(rows_ref[pl.ds(h, 1), :], (SUB, depth))
        band_ref[pl.ds(h * SUB, SUB), :] = pltpu.roll(row, 0, 1, stride=1, stride_axis=0).astype(jnp.bfloat16)
    even = parity_ref[0] == 0
    near, far = near_ref[...], far_ref[...]
    before = jnp.where(even, far, near)
    after = jnp.where(even, near, far)
    for b in range(cells // SUB):
        pieces = []
        for c in range(planes):
            pieces += [before[c, b * SUB :, :], own_ref[c], after[c, : (b + 1) * SUB, :]]
        pieces.append(jnp.zeros((depth - planes * window, width), jnp.bfloat16))
        span = jnp.concatenate(pieces, axis=0)
        part = jnp.dot(band_ref[...], span, preferred_element_type=jnp.float32)
        for h in range(heights):
            read_ref[h, pl.ds(b * SUB, SUB), :] = part[h * SUB : (h + 1) * SUB, :]


def span_kernel(gains_ref, read_ref, velocity_ref):
    blocks = read_ref.shape[0]
    taps = gains_ref.shape[1]
    half = (taps - 1) // 2
    read = jnp.concatenate([read_ref[j] for j in range(blocks)], axis=1)
    total = gains_ref[0, half] * read
    for e in range(taps):
        if e != half:
            total = total + gains_ref[0, e] * pltpu.roll(read, (half - e) % read.shape[1], 1)
    velocity_ref[0] = total


def local(wall_history, kernel_taps, span_gains):
    snaps, chans, cells, width = wall_history.shape
    taps = kernel_taps.shape[-1]
    planes = snaps * chans
    window = taps - 1 + SUB
    groups = lax.axis_size("ha")
    count = lax.axis_size("gx")
    depth = -(-planes * window // 128) * 128
    own = wall_history.reshape(planes, cells, width)
    far = lax.ppermute(own, "gx", [(i, (i - 1 if i % 2 == 0 else i + 1) % count) for i in range(count)])
    near = lax.ppermute(own, "gx", [(i, i ^ 1) for i in range(count)])
    rows = jnp.pad(kernel_taps.astype(jnp.float32).reshape(planes, taps), ((0, 0), (0, window - taps))).reshape(1, planes * window)
    rows = jnp.pad(rows, ((0, 0), (0, depth - planes * window)))
    rows = lax.all_to_all(jnp.broadcast_to(rows, (groups, depth)), "ha", 0, 0, tiled=True)
    parity = (lax.axis_index("gx") % 2).astype(jnp.int32).reshape(1)
    read = pl.pallas_call(
        band_kernel,
        out_shape=jax.ShapeDtypeStruct((groups, cells, width), jnp.float32),
        in_specs=[pl.BlockSpec(memory_space=pltpu.SMEM)] + [pl.BlockSpec(memory_space=pltpu.VMEM)] * 4,
        out_specs=pl.BlockSpec(memory_space=pltpu.VMEM),
        scratch_shapes=[pltpu.VMEM((groups * SUB, depth), jnp.bfloat16)],
        compiler_params=pltpu.CompilerParams(vmem_limit_bytes=32 * 1024 * 1024),
        cost_estimate=pl.CostEstimate(flops=2 * groups * cells * width * planes * window, bytes_accessed=2 << 20, transcendentals=0),
    )(parity, rows, own, near, far)
    read = lax.all_to_all(read, "ha", 0, 0, tiled=True)
    block = 32
    return pl.pallas_call(
        span_kernel,
        grid=(cells // block,),
        out_shape=jax.ShapeDtypeStruct((1, cells, groups * width), jnp.float32),
        in_specs=[pl.BlockSpec(memory_space=pltpu.SMEM), pl.BlockSpec((groups, block, width), lambda i: (0, i, 0))],
        out_specs=pl.BlockSpec((1, block, groups * width), lambda i: (0, i, 0)),
        compiler_params=pltpu.CompilerParams(vmem_limit_bytes=32 * 1024 * 1024),
    )(span_gains, read)


def solution(mesh):
    in_specs = (P(None, None, "gx", "ha"), P("ha", None, None, None), P("ha", None))
    out_specs = P("ha", "gx", None)
    return jax.shard_map(local, mesh=mesh, in_specs=in_specs, out_specs=out_specs, check_vma=False)
```

```python
import jax
import jax.numpy as jnp
from jax import lax
from jax.experimental import pallas as pl
from jax.experimental.pallas import tpu as pltpu
from jax.sharding import PartitionSpec as P

SUB = 32
NOTES = 16
LEVELS = 30719.0
OFFSET = 120.0
LOG2E = 1.4426950408889634
TINY = 1.2e-38


def row_kernel(taps_ref, rows_ref):
    groups, _, depth = rows_ref.shape
    snaps, chans, taps = taps_ref.shape
    pieces = []
    for s in range(snaps):
        for c in range(chans):
            pieces += [taps_ref[s, c : c + 1, :].astype(jnp.float32), jnp.zeros((1, SUB - 1), jnp.float32)]
    pieces.append(jnp.zeros((1, depth - snaps * chans * (taps + SUB - 1)), jnp.float32))
    row = jnp.concatenate(pieces, axis=1)
    for h in range(groups):
        rows_ref[h] = row


def gains_kernel(gains_ref, wide_ref):
    for e in range(gains_ref.shape[1]):
        wide_ref[e] = jnp.broadcast_to(gains_ref[0:1, e : e + 1], wide_ref.shape[1:])


def band_kernel(rows_ref, band_ref):
    heights, _, depth = rows_ref.shape
    for h in range(heights):
        row = jnp.broadcast_to(rows_ref[h], (SUB, depth))
        band_ref[pl.ds(h * SUB, SUB), :] = pltpu.roll(row, 0, 1, stride=1, stride_axis=0).astype(jnp.bfloat16)


def coded(values):
    peak = jnp.max(jnp.abs(values), axis=0, keepdims=True) * (1 + 1 / 128)
    scale = jnp.maximum(peak.astype(jnp.bfloat16).astype(jnp.float32), TINY)
    level = jnp.floor(jnp.abs(values) * (1.0 / scale) * LEVELS + 0.5) * (1 / 128)
    octave = jnp.floor(level)
    size = (level - octave + 1.0) * jnp.exp2(octave - OFFSET)
    return jnp.where(values < 0, -size, size).astype(jnp.bfloat16), scale


def decoded(code, scale):
    code = code.astype(jnp.float32)
    size = jnp.abs(code)
    octave = jnp.floor(jnp.log(size) * LOG2E)
    level = (octave + (OFFSET - 1.0) + size * jnp.exp2(-octave)) * (scale * (128 / LEVELS))
    return jnp.where(code < 0, -level, level)


def read_kernel(even_ref, band_ref, own_ref, near_ref, far_ref, read_ref):
    planes, cells, width = own_ref.shape
    heights = read_ref.shape[0]
    depth = band_ref.shape[1]
    window = 2 * cells + SUB
    even = even_ref[0] == 1
    near, far = near_ref[...], far_ref[...]
    before = jnp.where(even, far, near)
    after = jnp.where(even, near, far)
    scales = [[] for _ in range(heights)]
    for b in range(cells // SUB):
        pieces = []
        for c in range(planes):
            pieces += [before[c, b * SUB :, :], own_ref[c], after[c, : (b + 1) * SUB, :]]
        pieces.append(jnp.zeros((depth - planes * window, width), jnp.bfloat16))
        part = jnp.dot(band_ref[...], jnp.concatenate(pieces, axis=0), preferred_element_type=jnp.float32)
        for h in range(heights):
            code, scale = coded(part[h * SUB : (h + 1) * SUB, :])
            read_ref[h, pl.ds(b * SUB, SUB), :] = code
            scales[h].append(scale)
    for h in range(heights):
        rest = jnp.ones((read_ref.shape[1] - cells - len(scales[h]), width), jnp.float32)
        read_ref[h, pl.ds(cells, read_ref.shape[1] - cells), :] = jnp.concatenate(scales[h] + [rest], axis=0).astype(jnp.bfloat16)


def span_kernel(gains_ref, read_ref, velocity_ref):
    blocks, height, width = read_ref.shape
    rows = velocity_ref.shape[1]
    cells = height - NOTES
    taps = gains_ref.shape[0]
    half = (taps - 1) // 2
    at = pl.multiple_of(pl.program_id(0) * rows, rows)
    chosen = lax.broadcasted_iota(jnp.int32, (NOTES, width), 0) == pl.program_id(0)
    parts = []
    for j in range(blocks):
        scale = jnp.sum(jnp.where(chosen, read_ref[j, pl.ds(cells, NOTES), :].astype(jnp.float32), 0.0), axis=0, keepdims=True)
        parts.append(decoded(read_ref[j, pl.ds(at, rows), :], scale))
    read = jnp.concatenate(parts, axis=1)
    shape = (rows, read.shape[1])
    total = jnp.zeros(shape, jnp.float32)
    for e in range(taps):
        gain = jnp.broadcast_to(gains_ref[e, 0:1, 0:1], shape)
        total = total + gain * (read if e == half else pltpu.roll(read, (half - e) % read.shape[1], 1))
    velocity_ref[0] = total


def tied(value, *after):
    return lax.optimization_barrier((value, *after))[0]


def local(wall_history, kernel_taps, span_gains):
    snaps, chans, cells, width = wall_history.shape
    taps = kernel_taps.shape[-1]
    planes = snaps * chans
    window = taps - 1 + SUB
    groups = lax.axis_size("ha")
    count = lax.axis_size("gx")
    depth = -(-planes * window // 128) * 128
    vmem, smem = pl.BlockSpec(memory_space=pltpu.VMEM), pl.BlockSpec(memory_space=pltpu.SMEM)
    params = pltpu.CompilerParams(vmem_limit_bytes=32 * 1024 * 1024)
    long = pl.CostEstimate(flops=40_000_000_000, bytes_accessed=1 << 16, transcendentals=0)

    rows = pl.pallas_call(
        row_kernel,
        out_shape=jax.ShapeDtypeStruct((groups, 1, depth), jnp.float32),
        in_specs=[vmem],
        out_specs=vmem,
        compiler_params=params,
    )(kernel_taps.reshape(snaps, chans, taps))
    own = tied(wall_history.reshape(planes, cells, width), rows)
    rows = lax.all_to_all(rows, "ha", 0, 0, tiled=True)
    far = lax.ppermute(own, "gx", [(i, (i - 1 if i % 2 == 0 else i + 1) % count) for i in range(count)])
    near = lax.ppermute(own, "gx", [(i, i ^ 1) for i in range(count)])
    wide = pl.pallas_call(
        gains_kernel,
        out_shape=jax.ShapeDtypeStruct((span_gains.shape[1], 8, 128), jnp.float32),
        in_specs=[vmem],
        out_specs=vmem,
        compiler_params=params,
        cost_estimate=long,
    )(span_gains)
    band = pl.pallas_call(
        band_kernel,
        out_shape=jax.ShapeDtypeStruct((groups * SUB, depth), jnp.bfloat16),
        in_specs=[vmem],
        out_specs=vmem,
        compiler_params=params,
    )(tied(rows, wide))
    even = (lax.axis_index("gx") % 2 == 0).astype(jnp.int32).reshape(1)
    read = pl.pallas_call(
        read_kernel,
        out_shape=jax.ShapeDtypeStruct((groups, cells + NOTES, width), jnp.bfloat16),
        in_specs=[smem] + [vmem] * 4,
        out_specs=vmem,
        compiler_params=params,
        cost_estimate=pl.CostEstimate(flops=2 * groups * cells * width * planes * window, bytes_accessed=2 << 20, transcendentals=0),
    )(even, band, own, near, far)
    read = lax.all_to_all(read, "ha", 0, 0, tiled=True)
    return pl.pallas_call(
        span_kernel,
        grid=(cells // SUB,),
        out_shape=jax.ShapeDtypeStruct((1, cells, groups * width), jnp.float32),
        in_specs=[vmem, vmem],
        out_specs=pl.BlockSpec((1, SUB, groups * width), lambda i: (0, i, 0)),
        compiler_params=params,
    )(wide, read)


def solution(mesh):
    in_specs = (P(None, None, "gx", "ha"), P("ha", None, None, None), P("ha", None))
    out_specs = P("ha", "gx", None)
    return jax.shard_map(local, mesh=mesh, in_specs=in_specs, out_specs=out_specs, check_vma=False)
```

```python
import jax
import jax.numpy as jnp
from jax import lax
from jax.experimental import pallas as pl
from jax.experimental.pallas import tpu as pltpu
from jax.sharding import PartitionSpec as P

SUB = 32
NOTES = 16
LEVELS = 30719.0
OFFSET = 120.0
LOG2E = 1.4426950408889634
TINY = 1.2e-38


def gains_kernel(gains_ref, wide_ref):
    for e in range(gains_ref.shape[1]):
        wide_ref[e] = jnp.broadcast_to(gains_ref[0:1, e : e + 1], wide_ref.shape[1:])


def band_kernel(taps_ref, band_ref):
    heights, snaps, chans, taps = taps_ref.shape
    depth = band_ref.shape[1]
    for h in range(heights):
        pieces = []
        for s in range(snaps):
            for c in range(chans):
                pieces += [taps_ref[h, s, c : c + 1, :].astype(jnp.float32), jnp.zeros((1, SUB - 1), jnp.float32)]
        pieces.append(jnp.zeros((1, depth - snaps * chans * (taps + SUB - 1)), jnp.float32))
        row = jnp.broadcast_to(jnp.concatenate(pieces, axis=1), (SUB, depth))
        band_ref[pl.ds(h * SUB, SUB), :] = pltpu.roll(row, 0, 1, stride=1, stride_axis=0).astype(jnp.bfloat16)


def coded(values):
    peak = jnp.max(jnp.abs(values), axis=0, keepdims=True) * (1 + 1 / 128)
    scale = jnp.maximum(peak.astype(jnp.bfloat16).astype(jnp.float32), TINY)
    level = jnp.floor(jnp.abs(values) * (1.0 / scale) * LEVELS + 0.5) * (1 / 128)
    octave = jnp.floor(level)
    size = (level - octave + 1.0) * jnp.exp2(octave - OFFSET)
    return jnp.where(values < 0, -size, size).astype(jnp.bfloat16), scale


def decoded(code, scale):
    code = code.astype(jnp.float32)
    size = jnp.abs(code)
    octave = jnp.floor(jnp.log(size) * LOG2E)
    level = (octave + (OFFSET - 1.0) + size * jnp.exp2(-octave)) * (scale * (128 / LEVELS))
    return jnp.where(code < 0, -level, level)


def read_kernel(even_ref, band_ref, own_ref, near_ref, far_ref, read_ref):
    planes, cells, width = own_ref.shape
    heights = read_ref.shape[0]
    depth = band_ref.shape[1]
    window = 2 * cells + SUB
    even = even_ref[0] == 1
    near, far = near_ref[...], far_ref[...]
    before = jnp.where(even, far, near)
    after = jnp.where(even, near, far)
    scales = [[] for _ in range(heights)]
    for b in range(0, cells // SUB, 2):
        spans = []
        for at in (b * SUB, (b + 1) * SUB):
            pieces = []
            for c in range(planes):
                pieces += [before[c, at:, :], own_ref[c], after[c, : at + SUB, :]]
            pieces.append(jnp.zeros((depth - planes * window, width), jnp.bfloat16))
            spans.append(jnp.concatenate(pieces, axis=0))
        part = jnp.dot(band_ref[...], jnp.concatenate(spans, axis=1), preferred_element_type=jnp.float32)
        for h in range(heights):
            for k in range(2):
                code, scale = coded(part[h * SUB : (h + 1) * SUB, k * width : (k + 1) * width])
                read_ref[h, pl.ds((b + k) * SUB, SUB), :] = code
                scales[h].append(scale)
    for h in range(heights):
        rest = jnp.ones((read_ref.shape[1] - cells - len(scales[h]), width), jnp.float32)
        read_ref[h, pl.ds(cells, read_ref.shape[1] - cells), :] = jnp.concatenate(scales[h] + [rest], axis=0).astype(jnp.bfloat16)


def span_kernel(gains_ref, read_ref, velocity_ref):
    blocks, height, width = read_ref.shape
    rows = velocity_ref.shape[1]
    cells = height - NOTES
    at = pl.multiple_of(pl.program_id(0) * rows, rows)
    chosen = lax.broadcasted_iota(jnp.int32, (NOTES, width), 0) == pl.program_id(0)
    parts = []
    for j in range(blocks):
        scale = jnp.sum(jnp.where(chosen, read_ref[j, pl.ds(cells, NOTES), :].astype(jnp.float32), 0.0), axis=0, keepdims=True)
        parts.append(decoded(read_ref[j, pl.ds(at, rows), :], scale))
    read = jnp.concatenate(parts, axis=1)
    shape = (rows, read.shape[1])
    shifted = [pltpu.roll(read, 1, 1), read, pltpu.roll(read, shape[1] - 1, 1)]
    total = 0.0
    for k in range(3):
        third = 0.0
        for e in range(3):
            third = third + jnp.broadcast_to(gains_ref[3 * k + e, 0:1, 0:1], shape) * shifted[e]
        total = total + (third if k == 1 else pltpu.roll(third, (3 - 3 * k) % shape[1], 1))
    velocity_ref[0] = total


def tap_groups(count, groups):
    step = count // 2
    return [[(g if h < groups // 2 else g ^ step) * groups + h for h in range(groups)] for g in range(count)]


def tied(value, *after):
    return lax.optimization_barrier((value, *after))[0]


def local(wall_history, kernel_taps, span_gains):
    snaps, chans, cells, width = wall_history.shape
    taps = kernel_taps.shape[-1]
    planes = snaps * chans
    window = taps - 1 + SUB
    groups = lax.axis_size("ha")
    count = lax.axis_size("gx")
    depth = -(-planes * window // 128) * 128
    vmem, smem = pl.BlockSpec(memory_space=pltpu.VMEM), pl.BlockSpec(memory_space=pltpu.SMEM)
    params = pltpu.CompilerParams(vmem_limit_bytes=32 * 1024 * 1024)
    long = pl.CostEstimate(flops=40_000_000_000, bytes_accessed=1 << 16, transcendentals=0)

    rows = jnp.broadcast_to(kernel_taps, (groups, snaps, chans, taps))
    own = tied(wall_history.reshape(planes, cells, width), rows)
    rows = lax.all_to_all(rows, ("gx", "ha"), 0, 0, tiled=True, axis_index_groups=tap_groups(count, groups))
    far = lax.ppermute(own, "gx", [(i, (i - 1 if i % 2 == 0 else i + 1) % count) for i in range(count)])
    near = lax.ppermute(own, "gx", [(i, i ^ 1) for i in range(count)])
    wide = pl.pallas_call(
        gains_kernel,
        out_shape=jax.ShapeDtypeStruct((span_gains.shape[1], 8, 128), jnp.float32),
        in_specs=[vmem],
        out_specs=vmem,
        compiler_params=params,
        cost_estimate=long,
    )(span_gains)
    band = pl.pallas_call(
        band_kernel,
        out_shape=jax.ShapeDtypeStruct((groups * SUB, depth), jnp.bfloat16),
        in_specs=[vmem],
        out_specs=vmem,
        compiler_params=params,
    )(tied(rows, wide))
    even = (lax.axis_index("gx") % 2 == 0).astype(jnp.int32).reshape(1)
    read = pl.pallas_call(
        read_kernel,
        out_shape=jax.ShapeDtypeStruct((groups, cells + NOTES, width), jnp.bfloat16),
        in_specs=[smem] + [vmem] * 4,
        out_specs=vmem,
        compiler_params=params,
        cost_estimate=pl.CostEstimate(flops=2 * groups * cells * width * planes * window, bytes_accessed=2 << 20, transcendentals=0),
    )(even, band, own, near, far)
    read = lax.all_to_all(read, "ha", 0, 0, tiled=True)
    return pl.pallas_call(
        span_kernel,
        grid=(cells // SUB,),
        out_shape=jax.ShapeDtypeStruct((1, cells, groups * width), jnp.float32),
        in_specs=[vmem, vmem],
        out_specs=pl.BlockSpec((1, SUB, groups * width), lambda i: (0, i, 0)),
        compiler_params=params,
    )(wide, read)


def solution(mesh):
    in_specs = (P(None, None, "gx", "ha"), P("ha", None, None, None), P("ha", None))
    out_specs = P("ha", "gx", None)
    return jax.shard_map(local, mesh=mesh, in_specs=in_specs, out_specs=out_specs, check_vma=False)
```

```python
import jax
import jax.numpy as jnp
from jax import lax
from jax.experimental import pallas as pl
from jax.experimental.pallas import tpu as pltpu
from jax.sharding import PartitionSpec as P

SUB = 32
NOTES = 16
STEP = 64
LEVELS = 30719.0
OFFSET = 120.0
LOG2E = 1.4426950408889634
TINY = 2.0**-125


def gains_kernel(gains_ref, wide_ref):
    for e in range(gains_ref.shape[1]):
        wide_ref[e] = jnp.broadcast_to(gains_ref[0:1, e : e + 1], wide_ref.shape[1:])


def band_kernel(taps_ref, band_ref):
    heights, snaps, chans, taps = taps_ref.shape
    depth = band_ref.shape[1]
    for h in range(heights):
        pieces = []
        for s in range(snaps):
            for c in range(chans):
                pieces += [taps_ref[h, s, c : c + 1, :].astype(jnp.float32), jnp.zeros((1, SUB - 1), jnp.float32)]
        pieces.append(jnp.zeros((1, depth - snaps * chans * (taps + SUB - 1)), jnp.float32))
        row = jnp.broadcast_to(jnp.concatenate(pieces, axis=1), (SUB, depth))
        band_ref[pl.ds(h * SUB, SUB), :] = pltpu.roll(row, 0, 1, stride=1, stride_axis=0).astype(jnp.bfloat16)


def coded(values):
    peak = jnp.max(jnp.abs(values), axis=0, keepdims=True) * (1 + 1 / 128)
    scale = jnp.maximum(peak.astype(jnp.bfloat16).astype(jnp.float32), TINY)
    level = jnp.floor(jnp.abs(values) * (1.0 / scale) * LEVELS + 0.5) * (1 / 128)
    octave = jnp.floor(level)
    size = (level - octave + 1.0) * jnp.exp2(octave - OFFSET)
    return jnp.where(values < 0, -size, size).astype(jnp.bfloat16), scale


def decoded(code, scale):
    code = code.astype(jnp.float32)
    size = jnp.abs(code)
    octave = jnp.floor(jnp.log(size) * LOG2E)
    level = (octave + (OFFSET - 1.0) + size * jnp.exp2(-octave)) * (scale * (128 / LEVELS))
    return jnp.where(code < 0, -level, level)


def read_kernel(even_ref, band_ref, own_ref, near_ref, far_ref, read_ref):
    planes, cells, width = own_ref.shape
    heights = read_ref.shape[0]
    depth = band_ref.shape[1]
    window = 2 * cells + SUB
    even = even_ref[0] == 1
    near, far = near_ref[...], far_ref[...]
    before = jnp.where(even, far, near)
    after = jnp.where(even, near, far)
    scales = [[] for _ in range(heights)]
    for b in range(0, cells // SUB, 2):
        spans = []
        for at in (b * SUB, (b + 1) * SUB):
            pieces = []
            for c in range(planes):
                pieces += [before[c, at:, :], own_ref[c], after[c, : at + SUB, :]]
            pieces.append(jnp.zeros((depth - planes * window, width), jnp.bfloat16))
            spans.append(jnp.concatenate(pieces, axis=0))
        part = jnp.dot(band_ref[...], jnp.concatenate(spans, axis=1), preferred_element_type=jnp.float32)
        for h in range(heights):
            for k in range(2):
                code, scale = coded(part[h * SUB : (h + 1) * SUB, k * width : (k + 1) * width])
                read_ref[h, pl.ds((b + k) * SUB, SUB), :] = code
                scales[h].append(scale)
    for h in range(heights):
        rest = jnp.ones((read_ref.shape[1] - cells - len(scales[h]), width), jnp.float32)
        read_ref[h, pl.ds(cells, read_ref.shape[1] - cells), :] = jnp.concatenate(scales[h] + [rest], axis=0).astype(jnp.bfloat16)


def span_kernel(gains_ref, read_ref, velocity_ref):
    blocks, height, width = read_ref.shape
    rows = velocity_ref.shape[1]
    cells = height - NOTES
    at = pl.multiple_of(pl.program_id(0) * rows, rows)
    index = lax.broadcasted_iota(jnp.int32, (NOTES, width), 0)
    parts = []
    for j in range(blocks):
        notes = read_ref[j, pl.ds(cells, NOTES), :].astype(jnp.float32)
        pieces = []
        for k in range(rows // SUB):
            chosen = index == pl.program_id(0) * (rows // SUB) + k
            scale = jnp.sum(jnp.where(chosen, notes, 0.0), axis=0, keepdims=True)
            pieces.append(decoded(read_ref[j, pl.ds(at + k * SUB, SUB), :], scale))
        parts.append(jnp.concatenate(pieces, axis=0))
    read = jnp.concatenate(parts, axis=1)
    shape = (rows, read.shape[1])
    shifted = [pltpu.roll(read, 1, 1), read, pltpu.roll(read, shape[1] - 1, 1)]
    total = 0.0
    for k in range(3):
        third = 0.0
        for e in range(3):
            third = third + jnp.broadcast_to(gains_ref[3 * k + e, 0:1, 0:1], shape) * shifted[e]
        total = total + (third if k == 1 else pltpu.roll(third, (3 - 3 * k) % shape[1], 1))
    velocity_ref[0] = total


def tap_groups(count, groups):
    step = count // 2
    return [[(g if h < groups // 2 else g ^ step) * groups + h for h in range(groups)] for g in range(count)]


def tied(value, *after):
    return lax.optimization_barrier((value, *after))[0]


def local(wall_history, kernel_taps, span_gains):
    snaps, chans, cells, width = wall_history.shape
    taps = kernel_taps.shape[-1]
    planes = snaps * chans
    window = taps - 1 + SUB
    groups = lax.axis_size("ha")
    count = lax.axis_size("gx")
    depth = -(-planes * window // 128) * 128
    vmem, smem = pl.BlockSpec(memory_space=pltpu.VMEM), pl.BlockSpec(memory_space=pltpu.SMEM)
    params = pltpu.CompilerParams(vmem_limit_bytes=32 * 1024 * 1024)
    long = pl.CostEstimate(flops=40_000_000_000, bytes_accessed=1 << 16, transcendentals=0)

    rows = jnp.broadcast_to(kernel_taps, (groups, snaps, chans, taps))
    own = tied(wall_history.reshape(planes, cells, width), rows)
    rows = lax.all_to_all(rows, ("gx", "ha"), 0, 0, tiled=True, axis_index_groups=tap_groups(count, groups))
    far = lax.ppermute(own, "gx", [(i, (i - 1 if i % 2 == 0 else i + 1) % count) for i in range(count)])
    near = lax.ppermute(own, "gx", [(i, i ^ 1) for i in range(count)])
    wide = pl.pallas_call(
        gains_kernel,
        out_shape=jax.ShapeDtypeStruct((span_gains.shape[1], 8, 128), jnp.float32),
        in_specs=[vmem],
        out_specs=vmem,
        compiler_params=params,
        cost_estimate=long,
    )(span_gains)
    band = pl.pallas_call(
        band_kernel,
        out_shape=jax.ShapeDtypeStruct((groups * SUB, depth), jnp.bfloat16),
        in_specs=[vmem],
        out_specs=vmem,
        compiler_params=params,
    )(tied(rows, wide))
    even = (lax.axis_index("gx") % 2 == 0).astype(jnp.int32).reshape(1)
    read = pl.pallas_call(
        read_kernel,
        out_shape=jax.ShapeDtypeStruct((groups, cells + NOTES, width), jnp.bfloat16),
        in_specs=[smem] + [vmem] * 4,
        out_specs=vmem,
        compiler_params=params,
        cost_estimate=pl.CostEstimate(flops=2 * groups * cells * width * planes * window, bytes_accessed=2 << 20, transcendentals=0),
    )(even, band, own, near, far)
    read = lax.all_to_all(read, "ha", 0, 0, tiled=True)
    return pl.pallas_call(
        span_kernel,
        grid=(cells // STEP,),
        out_shape=jax.ShapeDtypeStruct((1, cells, groups * width), jnp.float32),
        in_specs=[vmem, vmem],
        out_specs=pl.BlockSpec((1, STEP, groups * width), lambda i: (0, i, 0)),
        compiler_params=params,
    )(wide, read)


def solution(mesh):
    in_specs = (P(None, None, "gx", "ha"), P("ha", None, None, None), P("ha", None))
    out_specs = P("ha", "gx", None)
    return jax.shard_map(local, mesh=mesh, in_specs=in_specs, out_specs=out_specs, check_vma=False)
```

```python
import jax
import jax.numpy as jnp
from jax import lax
from jax.experimental import pallas as pl
from jax.experimental.pallas import tpu as pltpu
from jax.sharding import PartitionSpec as P

SUB = 32
ORDER = (6, 7, 5, 4, 2, 3, 1, 0)
NOTES = 16
STEP = 64
LEVELS = 30719.0
OFFSET = 120.0
LOG2E = 1.4426950408889634
TINY = 2.0**-125


def gains_kernel(gains_ref, wide_ref):
    for e in range(gains_ref.shape[1]):
        wide_ref[e] = jnp.broadcast_to(gains_ref[0:1, e : e + 1], wide_ref.shape[1:])


def band_kernel(taps_ref, band_ref):
    heights, snaps, chans, taps = taps_ref.shape
    depth = band_ref.shape[1]
    for h in range(heights):
        pieces = []
        for s in range(snaps):
            for c in range(chans):
                pieces += [taps_ref[h, s, c : c + 1, :].astype(jnp.float32), jnp.zeros((1, SUB - 1), jnp.float32)]
        pieces.append(jnp.zeros((1, depth - snaps * chans * (taps + SUB - 1)), jnp.float32))
        row = jnp.broadcast_to(jnp.concatenate(pieces, axis=1), (SUB, depth))
        band_ref[pl.ds(h * SUB, SUB), :] = pltpu.roll(row, 0, 1, stride=1, stride_axis=0).astype(jnp.bfloat16)


def coded(values):
    peak = jnp.max(jnp.abs(values), axis=0, keepdims=True) * (1 + 1 / 128)
    scale = jnp.maximum(peak.astype(jnp.bfloat16).astype(jnp.float32), TINY)
    level = jnp.floor(jnp.abs(values) * (1.0 / scale) * LEVELS + 0.5) * (1 / 128)
    octave = jnp.floor(level)
    size = (level - octave + 1.0) * jnp.exp2(octave - OFFSET)
    return jnp.where(values < 0, -size, size).astype(jnp.bfloat16), scale


def decoded(code, scale):
    code = code.astype(jnp.float32)
    size = jnp.abs(code)
    octave = jnp.floor(jnp.log(size) * LOG2E)
    level = (octave + (OFFSET - 1.0) + size * jnp.exp2(-octave)) * (scale * (128 / LEVELS))
    return jnp.where(code < 0, -level, level)


def read_kernel(even_ref, band_ref, own_ref, near_ref, far_ref, read_ref):
    planes, cells, width = own_ref.shape
    heights = read_ref.shape[0]
    depth = band_ref.shape[1]
    window = 2 * cells + SUB
    even = even_ref[0] == 1
    near, far = near_ref[...], far_ref[...]
    before = jnp.where(even, far, near)
    after = jnp.where(even, near, far)
    scales = [[] for _ in range(heights)]
    for b in range(0, cells // SUB, 2):
        spans = []
        for at in (b * SUB, (b + 1) * SUB):
            pieces = []
            for c in range(planes):
                pieces += [before[c, at:, :], own_ref[c], after[c, : at + SUB, :]]
            pieces.append(jnp.zeros((depth - planes * window, width), jnp.bfloat16))
            spans.append(jnp.concatenate(pieces, axis=0))
        part = jnp.dot(band_ref[...], jnp.concatenate(spans, axis=1), preferred_element_type=jnp.float32)
        for h in range(heights):
            for k in range(2):
                code, scale = coded(part[h * SUB : (h + 1) * SUB, k * width : (k + 1) * width])
                read_ref[h, pl.ds((b + k) * SUB, SUB), :] = code
                scales[h].append(scale)
    for h in range(heights):
        rest = jnp.ones((read_ref.shape[1] - cells - len(scales[h]), width), jnp.float32)
        read_ref[h, pl.ds(cells, read_ref.shape[1] - cells), :] = jnp.concatenate(scales[h] + [rest], axis=0).astype(jnp.bfloat16)


def span_kernel(gains_ref, read_ref, velocity_ref):
    blocks, height, width = read_ref.shape
    rows = velocity_ref.shape[1]
    cells = height - NOTES
    at = pl.multiple_of(pl.program_id(0) * rows, rows)
    index = lax.broadcasted_iota(jnp.int32, (NOTES, width), 0)
    parts = []
    for j in (ORDER.index(block) for block in range(blocks)):
        notes = read_ref[j, pl.ds(cells, NOTES), :].astype(jnp.float32)
        pieces = []
        for k in range(rows // SUB):
            chosen = index == pl.program_id(0) * (rows // SUB) + k
            scale = jnp.sum(jnp.where(chosen, notes, 0.0), axis=0, keepdims=True)
            pieces.append(decoded(read_ref[j, pl.ds(at + k * SUB, SUB), :], scale))
        parts.append(jnp.concatenate(pieces, axis=0))
    read = jnp.concatenate(parts, axis=1)
    shape = (rows, read.shape[1])
    shifted = [pltpu.roll(read, 1, 1), read, pltpu.roll(read, shape[1] - 1, 1)]
    total = 0.0
    for k in range(3):
        third = 0.0
        for e in range(3):
            third = third + jnp.broadcast_to(gains_ref[3 * k + e, 0:1, 0:1], shape) * shifted[e]
        total = total + (third if k == 1 else pltpu.roll(third, (3 - 3 * k) % shape[1], 1))
    velocity_ref[0] = total


def tap_groups(count, groups):
    step = count // 2
    return [[(g if h < groups // 2 else g ^ step) * groups + h for h in ORDER] for g in range(count)]


def tied(value, *after):
    return lax.optimization_barrier((value, *after))[0]


def local(wall_history, kernel_taps, span_gains):
    snaps, chans, cells, width = wall_history.shape
    taps = kernel_taps.shape[-1]
    planes = snaps * chans
    window = taps - 1 + SUB
    groups = lax.axis_size("ha")
    count = lax.axis_size("gx")
    depth = -(-planes * window // 128) * 128
    vmem, smem = pl.BlockSpec(memory_space=pltpu.VMEM), pl.BlockSpec(memory_space=pltpu.SMEM)
    params = pltpu.CompilerParams(vmem_limit_bytes=32 * 1024 * 1024)
    long = pl.CostEstimate(flops=40_000_000_000, bytes_accessed=1 << 16, transcendentals=0)

    rows = jnp.broadcast_to(kernel_taps, (groups, snaps, chans, taps))
    own = tied(wall_history.reshape(planes, cells, width), rows)
    rows = lax.all_to_all(rows, ("gx", "ha"), 0, 0, tiled=True, axis_index_groups=tap_groups(count, groups))
    far = lax.ppermute(own, "gx", [(i, (i - 1 if i % 2 == 0 else i + 1) % count) for i in range(count)])
    near = lax.ppermute(own, "gx", [(i, i ^ 1) for i in range(count)])
    wide = pl.pallas_call(
        gains_kernel,
        out_shape=jax.ShapeDtypeStruct((span_gains.shape[1], 8, 128), jnp.float32),
        in_specs=[vmem],
        out_specs=vmem,
        compiler_params=params,
        cost_estimate=long,
    )(span_gains)
    band = pl.pallas_call(
        band_kernel,
        out_shape=jax.ShapeDtypeStruct((groups * SUB, depth), jnp.bfloat16),
        in_specs=[vmem],
        out_specs=vmem,
        compiler_params=params,
    )(tied(rows, wide))
    even = (lax.axis_index("gx") % 2 == 0).astype(jnp.int32).reshape(1)
    read = pl.pallas_call(
        read_kernel,
        out_shape=jax.ShapeDtypeStruct((groups, cells + NOTES, width), jnp.bfloat16),
        in_specs=[smem] + [vmem] * 4,
        out_specs=vmem,
        compiler_params=params,
        cost_estimate=pl.CostEstimate(flops=2 * groups * cells * width * planes * window, bytes_accessed=2 << 20, transcendentals=0),
    )(even, band, own, near, far)
    read = lax.all_to_all(read, "ha", 0, 0, tiled=True, axis_index_groups=[list(ORDER)])
    return pl.pallas_call(
        span_kernel,
        grid=(cells // STEP,),
        out_shape=jax.ShapeDtypeStruct((1, cells, groups * width), jnp.float32),
        in_specs=[vmem, vmem],
        out_specs=pl.BlockSpec((1, STEP, groups * width), lambda i: (0, i, 0)),
        compiler_params=params,
    )(wide, read)


def solution(mesh):
    in_specs = (P(None, None, "gx", "ha"), P("ha", None, None, None), P("ha", None))
    out_specs = P("ha", "gx", None)
    return jax.shard_map(local, mesh=mesh, in_specs=in_specs, out_specs=out_specs, check_vma=False)
```

```python
import jax
import jax.numpy as jnp
from jax import lax
from jax.experimental import pallas as pl
from jax.experimental.pallas import tpu as pltpu
from jax.sharding import PartitionSpec as P

SUB = 32
ORDER = (4, 5, 6, 7, 0, 1, 2, 3)
TAP_ORDER = (6, 7, 5, 4, 2, 3, 1, 0)
NOTES = 16
STEP = 64
LEVELS = 30719.0
OFFSET = 120.0
LOG2E = 1.4426950408889634
TINY = 2.0**-125


def gains_kernel(gains_ref, wide_ref):
    for e in range(gains_ref.shape[1]):
        wide_ref[e] = jnp.broadcast_to(gains_ref[0:1, e : e + 1], wide_ref.shape[1:])


def band_kernel(taps_ref, band_ref):
    heights, snaps, chans, taps = taps_ref.shape
    depth = band_ref.shape[1]
    for h in range(heights):
        pieces = []
        for s in range(snaps):
            for c in range(chans):
                pieces += [taps_ref[h, s, c : c + 1, :].astype(jnp.float32), jnp.zeros((1, SUB - 1), jnp.float32)]
        pieces.append(jnp.zeros((1, depth - snaps * chans * (taps + SUB - 1)), jnp.float32))
        row = jnp.broadcast_to(jnp.concatenate(pieces, axis=1), (SUB, depth))
        band_ref[pl.ds(ORDER.index(TAP_ORDER[h]) * SUB, SUB), :] = pltpu.roll(row, 0, 1, stride=1, stride_axis=0).astype(jnp.bfloat16)


def coded(values):
    peak = jnp.max(jnp.abs(values), axis=0, keepdims=True) * (1 + 1 / 128)
    scale = jnp.maximum(peak.astype(jnp.bfloat16).astype(jnp.float32), TINY)
    level = jnp.floor(jnp.abs(values) * (1.0 / scale) * LEVELS + 0.5) * (1 / 128)
    octave = jnp.floor(level)
    size = (level - octave + 1.0) * jnp.exp2(octave - OFFSET)
    return jnp.where(values < 0, -size, size).astype(jnp.bfloat16), scale


def decoded(code, scale):
    code = code.astype(jnp.float32)
    size = jnp.abs(code)
    octave = jnp.floor(jnp.log(size) * LOG2E)
    level = (octave + (OFFSET - 1.0) + size * jnp.exp2(-octave)) * (scale * (128 / LEVELS))
    return jnp.where(code < 0, -level, level)


def read_kernel(even_ref, band_ref, own_ref, near_ref, far_ref, read_ref):
    planes, cells, width = own_ref.shape
    heights = read_ref.shape[0]
    depth = band_ref.shape[1]
    window = 2 * cells + SUB
    even = even_ref[0] == 1
    near, far = near_ref[...], far_ref[...]
    before = jnp.where(even, far, near)
    after = jnp.where(even, near, far)
    scales = [[] for _ in range(heights)]
    for b in range(0, cells // SUB, 2):
        spans = []
        for at in (b * SUB, (b + 1) * SUB):
            pieces = []
            for c in range(planes):
                pieces += [before[c, at:, :], own_ref[c], after[c, : at + SUB, :]]
            pieces.append(jnp.zeros((depth - planes * window, width), jnp.bfloat16))
            spans.append(jnp.concatenate(pieces, axis=0))
        part = jnp.dot(band_ref[...], jnp.concatenate(spans, axis=1), preferred_element_type=jnp.float32)
        for h in range(heights):
            for k in range(2):
                code, scale = coded(part[h * SUB : (h + 1) * SUB, k * width : (k + 1) * width])
                read_ref[h, pl.ds((b + k) * SUB, SUB), :] = code
                scales[h].append(scale)
    for h in range(heights):
        rest = jnp.ones((read_ref.shape[1] - cells - len(scales[h]), width), jnp.float32)
        read_ref[h, pl.ds(cells, read_ref.shape[1] - cells), :] = jnp.concatenate(scales[h] + [rest], axis=0).astype(jnp.bfloat16)


def span_kernel(gains_ref, read_ref, velocity_ref):
    blocks, height, width = read_ref.shape
    rows = velocity_ref.shape[1]
    cells = height - NOTES
    at = pl.multiple_of(pl.program_id(0) * rows, rows)
    index = lax.broadcasted_iota(jnp.int32, (NOTES, width), 0)
    parts = []
    for j in (ORDER.index(block) for block in range(blocks)):
        notes = read_ref[j, pl.ds(cells, NOTES), :].astype(jnp.float32)
        pieces = []
        for k in range(rows // SUB):
            chosen = index == pl.program_id(0) * (rows // SUB) + k
            scale = jnp.sum(jnp.where(chosen, notes, 0.0), axis=0, keepdims=True)
            pieces.append(decoded(read_ref[j, pl.ds(at + k * SUB, SUB), :], scale))
        parts.append(jnp.concatenate(pieces, axis=0))
    read = jnp.concatenate(parts, axis=1)
    shape = (rows, read.shape[1])
    shifted = [pltpu.roll(read, 1, 1), read, pltpu.roll(read, shape[1] - 1, 1)]
    total = 0.0
    for k in range(3):
        third = 0.0
        for e in range(3):
            third = third + jnp.broadcast_to(gains_ref[3 * k + e, 0:1, 0:1], shape) * shifted[e]
        total = total + (third if k == 1 else pltpu.roll(third, (3 - 3 * k) % shape[1], 1))
    velocity_ref[0] = total


def tap_groups(count, groups):
    step = count // 2
    return [[(g if h < groups // 2 else g ^ step) * groups + h for h in TAP_ORDER] for g in range(count)]


def tied(value, *after):
    return lax.optimization_barrier((value, *after))[0]


def local(wall_history, kernel_taps, span_gains):
    snaps, chans, cells, width = wall_history.shape
    taps = kernel_taps.shape[-1]
    planes = snaps * chans
    window = taps - 1 + SUB
    groups = lax.axis_size("ha")
    count = lax.axis_size("gx")
    depth = -(-planes * window // 128) * 128
    vmem, smem = pl.BlockSpec(memory_space=pltpu.VMEM), pl.BlockSpec(memory_space=pltpu.SMEM)
    params = pltpu.CompilerParams(vmem_limit_bytes=32 * 1024 * 1024)
    long = pl.CostEstimate(flops=40_000_000_000, bytes_accessed=1 << 16, transcendentals=0)

    rows = jnp.broadcast_to(kernel_taps, (groups, snaps, chans, taps))
    own = tied(wall_history.reshape(planes, cells, width), rows)
    rows = lax.all_to_all(rows, ("gx", "ha"), 0, 0, tiled=True, axis_index_groups=tap_groups(count, groups))
    far = lax.ppermute(own, "gx", [(i, (i - 1 if i % 2 == 0 else i + 1) % count) for i in range(count)])
    near = lax.ppermute(own, "gx", [(i, i ^ 1) for i in range(count)])
    wide = pl.pallas_call(
        gains_kernel,
        out_shape=jax.ShapeDtypeStruct((span_gains.shape[1], 8, 128), jnp.float32),
        in_specs=[vmem],
        out_specs=vmem,
        compiler_params=params,
        cost_estimate=long,
    )(span_gains)
    band = pl.pallas_call(
        band_kernel,
        out_shape=jax.ShapeDtypeStruct((groups * SUB, depth), jnp.bfloat16),
        in_specs=[vmem],
        out_specs=vmem,
        compiler_params=params,
    )(tied(rows, wide))
    even = (lax.axis_index("gx") % 2 == 0).astype(jnp.int32).reshape(1)
    read = pl.pallas_call(
        read_kernel,
        out_shape=jax.ShapeDtypeStruct((groups, cells + NOTES, width), jnp.bfloat16),
        in_specs=[smem] + [vmem] * 4,
        out_specs=vmem,
        compiler_params=params,
        cost_estimate=pl.CostEstimate(flops=2 * groups * cells * width * planes * window, bytes_accessed=2 << 20, transcendentals=0),
    )(even, band, own, near, far)
    read = lax.all_to_all(read, "ha", 0, 0, tiled=True, axis_index_groups=[list(ORDER)])
    return pl.pallas_call(
        span_kernel,
        grid=(cells // STEP,),
        out_shape=jax.ShapeDtypeStruct((1, cells, groups * width), jnp.float32),
        in_specs=[vmem, vmem],
        out_specs=pl.BlockSpec((1, STEP, groups * width), lambda i: (0, i, 0)),
        compiler_params=params,
    )(wide, read)


def solution(mesh):
    in_specs = (P(None, None, "gx", "ha"), P("ha", None, None, None), P("ha", None))
    out_specs = P("ha", "gx", None)
    return jax.shard_map(local, mesh=mesh, in_specs=in_specs, out_specs=out_specs, check_vma=False)
```

```python
import jax
import jax.numpy as jnp
from jax import lax
from jax.experimental import pallas as pl
from jax.experimental.pallas import tpu as pltpu
from jax.sharding import PartitionSpec as P

SUB = 16
ORDER = (4, 5, 6, 7, 0, 1, 2, 3)
TAP_ORDER = (6, 7, 5, 4, 2, 3, 1, 0)
NOTES = 16
STEP = 64
LEVELS = 30719.0
OFFSET = 120.0
LOG2E = 1.4426950408889634
TINY = 2.0**-125


def gains_kernel(gains_ref, wide_ref):
    for e in range(gains_ref.shape[1]):
        wide_ref[e] = jnp.broadcast_to(gains_ref[0:1, e : e + 1], wide_ref.shape[1:])


def band_kernel(taps_ref, band_ref):
    heights, snaps, chans, taps = taps_ref.shape
    depth = band_ref.shape[1]
    for h in range(heights):
        pieces = []
        for s in range(snaps):
            for c in range(chans):
                pieces += [taps_ref[h, s, c : c + 1, :].astype(jnp.float32), jnp.zeros((1, SUB - 1), jnp.float32)]
        pieces.append(jnp.zeros((1, depth - snaps * chans * (taps + SUB - 1)), jnp.float32))
        row = jnp.broadcast_to(jnp.concatenate(pieces, axis=1), (SUB, depth))
        band_ref[pl.ds(ORDER.index(TAP_ORDER[h]) * SUB, SUB), :] = pltpu.roll(row, 0, 1, stride=1, stride_axis=0).astype(jnp.bfloat16)


def coded(values):
    peak = jnp.max(jnp.abs(values), axis=0, keepdims=True) * (1 + 1 / 128)
    scale = jnp.maximum(peak.astype(jnp.bfloat16).astype(jnp.float32), TINY)
    level = jnp.floor(jnp.abs(values) * (1.0 / scale) * LEVELS + 0.5) * (1 / 128)
    octave = jnp.floor(level)
    size = (level - octave + 1.0) * jnp.exp2(octave - OFFSET)
    return jnp.where(values < 0, -size, size).astype(jnp.bfloat16), scale


def decoded(code, scale):
    code = code.astype(jnp.float32)
    size = jnp.abs(code)
    octave = jnp.floor(jnp.log(size) * LOG2E)
    level = (octave + (OFFSET - 1.0) + size * jnp.exp2(-octave)) * (scale * (128 / LEVELS))
    return jnp.where(code < 0, -level, level)


def read_kernel(even_ref, band_ref, own_ref, near_ref, far_ref, read_ref):
    planes, cells, width = own_ref.shape
    heights = read_ref.shape[0]
    depth = band_ref.shape[1]
    window = 2 * cells + SUB
    even = even_ref[0] == 1
    near, far = near_ref[...], far_ref[...]
    before = jnp.where(even, far, near)
    after = jnp.where(even, near, far)
    scales = [[] for _ in range(heights)]
    for b in range(0, cells // SUB, 2):
        spans = []
        for at in (b * SUB, (b + 1) * SUB):
            pieces = []
            for c in range(planes):
                pieces += [before[c, at:, :], own_ref[c], after[c, : at + SUB, :]]
            pieces.append(jnp.zeros((depth - planes * window, width), jnp.bfloat16))
            spans.append(jnp.concatenate(pieces, axis=0))
        part = jnp.dot(band_ref[...], jnp.concatenate(spans, axis=1), preferred_element_type=jnp.float32)
        for h in range(heights):
            for k in range(2):
                code, scale = coded(part[h * SUB : (h + 1) * SUB, k * width : (k + 1) * width])
                read_ref[h, pl.ds((b + k) * SUB, SUB), :] = code
                scales[h].append(scale)
    for h in range(heights):
        rest = jnp.ones((read_ref.shape[1] - cells - len(scales[h]), width), jnp.float32)
        read_ref[h, pl.ds(cells, read_ref.shape[1] - cells), :] = jnp.concatenate(scales[h] + [rest], axis=0).astype(jnp.bfloat16)


def span_kernel(gains_ref, read_ref, velocity_ref):
    blocks, height, width = read_ref.shape
    rows = velocity_ref.shape[1]
    cells = height - NOTES
    at = pl.multiple_of(pl.program_id(0) * rows, rows)
    index = lax.broadcasted_iota(jnp.int32, (NOTES, width), 0)
    parts = []
    for j in (ORDER.index(block) for block in range(blocks)):
        notes = read_ref[j, pl.ds(cells, NOTES), :].astype(jnp.float32)
        pieces = []
        for k in range(rows // SUB):
            chosen = index == pl.program_id(0) * (rows // SUB) + k
            scale = jnp.sum(jnp.where(chosen, notes, 0.0), axis=0, keepdims=True)
            pieces.append(decoded(read_ref[j, pl.ds(at + k * SUB, SUB), :], scale))
        parts.append(jnp.concatenate(pieces, axis=0))
    read = jnp.concatenate(parts, axis=1)
    shape = (rows, read.shape[1])
    shifted = [pltpu.roll(read, 1, 1), read, pltpu.roll(read, shape[1] - 1, 1)]
    total = 0.0
    for k in range(3):
        third = 0.0
        for e in range(3):
            third = third + jnp.broadcast_to(gains_ref[3 * k + e, 0:1, 0:1], shape) * shifted[e]
        total = total + (third if k == 1 else pltpu.roll(third, (3 - 3 * k) % shape[1], 1))
    velocity_ref[0] = total


def tap_groups(count, groups):
    step = count // 2
    return [[(g if h < groups // 2 else g ^ step) * groups + h for h in TAP_ORDER] for g in range(count)]


def tied(value, *after):
    return lax.optimization_barrier((value, *after))[0]


def local(wall_history, kernel_taps, span_gains):
    snaps, chans, cells, width = wall_history.shape
    taps = kernel_taps.shape[-1]
    planes = snaps * chans
    window = taps - 1 + SUB
    groups = lax.axis_size("ha")
    count = lax.axis_size("gx")
    depth = -(-planes * window // 128) * 128
    vmem, smem = pl.BlockSpec(memory_space=pltpu.VMEM), pl.BlockSpec(memory_space=pltpu.SMEM)
    params = pltpu.CompilerParams(vmem_limit_bytes=32 * 1024 * 1024)
    long = pl.CostEstimate(flops=40_000_000_000, bytes_accessed=1 << 16, transcendentals=0)

    rows = jnp.broadcast_to(kernel_taps, (groups, snaps, chans, taps))
    own = tied(wall_history.reshape(planes, cells, width), rows)
    rows = lax.all_to_all(rows, ("gx", "ha"), 0, 0, tiled=True, axis_index_groups=tap_groups(count, groups))
    far = lax.ppermute(own, "gx", [(i, (i - 1 if i % 2 == 0 else i + 1) % count) for i in range(count)])
    near = lax.ppermute(own, "gx", [(i, i ^ 1) for i in range(count)])
    wide = pl.pallas_call(
        gains_kernel,
        out_shape=jax.ShapeDtypeStruct((span_gains.shape[1], 8, 128), jnp.float32),
        in_specs=[vmem],
        out_specs=vmem,
        compiler_params=params,
        cost_estimate=long,
    )(span_gains)
    band = pl.pallas_call(
        band_kernel,
        out_shape=jax.ShapeDtypeStruct((groups * SUB, depth), jnp.bfloat16),
        in_specs=[vmem],
        out_specs=vmem,
        compiler_params=params,
    )(tied(rows, wide))
    even = (lax.axis_index("gx") % 2 == 0).astype(jnp.int32).reshape(1)
    read = pl.pallas_call(
        read_kernel,
        out_shape=jax.ShapeDtypeStruct((groups, cells + NOTES, width), jnp.bfloat16),
        in_specs=[smem] + [vmem] * 4,
        out_specs=vmem,
        compiler_params=params,
        cost_estimate=pl.CostEstimate(flops=2 * groups * cells * width * planes * window, bytes_accessed=2 << 20, transcendentals=0),
    )(even, band, own, near, far)
    read = lax.all_to_all(read, "ha", 0, 0, tiled=True, axis_index_groups=[list(ORDER)])
    return pl.pallas_call(
        span_kernel,
        grid=(cells // STEP,),
        out_shape=jax.ShapeDtypeStruct((1, cells, groups * width), jnp.float32),
        in_specs=[vmem, vmem],
        out_specs=pl.BlockSpec((1, STEP, groups * width), lambda i: (0, i, 0)),
        compiler_params=params,
    )(wide, read)


def solution(mesh):
    in_specs = (P(None, None, "gx", "ha"), P("ha", None, None, None), P("ha", None))
    out_specs = P("ha", "gx", None)
    return jax.shard_map(local, mesh=mesh, in_specs=in_specs, out_specs=out_specs, check_vma=False)
```

```python
import jax
import jax.numpy as jnp
from jax import lax
from jax.experimental import pallas as pl
from jax.experimental.pallas import tpu as pltpu
from jax.sharding import PartitionSpec as P

SUB = 16
ORDER = (4, 5, 6, 7, 3, 2, 1, 0)
TAP_ORDER = (6, 7, 5, 4, 2, 3, 1, 0)
NOTES = 16
STEP = 64
LEVELS = 30719.0
OFFSET = 120.0
LOG2E = 1.4426950408889634
TINY = 2.0**-125


def gains_kernel(gains_ref, wide_ref):
    for e in range(gains_ref.shape[1]):
        wide_ref[e] = jnp.broadcast_to(gains_ref[0:1, e : e + 1], wide_ref.shape[1:])


def band_kernel(taps_ref, band_ref):
    heights, snaps, chans, taps = taps_ref.shape
    depth = band_ref.shape[1]
    for h in range(heights):
        pieces = []
        for s in range(snaps):
            for c in range(chans):
                pieces += [taps_ref[h, s, c : c + 1, :].astype(jnp.float32), jnp.zeros((1, SUB - 1), jnp.float32)]
        pieces.append(jnp.zeros((1, depth - snaps * chans * (taps + SUB - 1)), jnp.float32))
        row = jnp.broadcast_to(jnp.concatenate(pieces, axis=1), (SUB, depth))
        band_ref[pl.ds(ORDER.index(TAP_ORDER[h]) * SUB, SUB), :] = pltpu.roll(row, 0, 1, stride=1, stride_axis=0).astype(jnp.bfloat16)


def coded(values):
    peak = jnp.max(jnp.abs(values), axis=0, keepdims=True) * (1 + 1 / 128)
    scale = jnp.maximum(peak.astype(jnp.bfloat16).astype(jnp.float32), TINY)
    level = jnp.floor(jnp.abs(values) * (1.0 / scale) * LEVELS + 0.5) * (1 / 128)
    octave = jnp.floor(level)
    size = (level - octave + 1.0) * jnp.exp2(octave - OFFSET)
    return jnp.where(values < 0, -size, size).astype(jnp.bfloat16), scale


def decoded(code, scale):
    code = code.astype(jnp.float32)
    size = jnp.abs(code)
    octave = jnp.floor(jnp.log(size) * LOG2E)
    level = (octave + (OFFSET - 1.0) + size * jnp.exp2(-octave)) * (scale * (128 / LEVELS))
    return jnp.where(code < 0, -level, level)


def read_kernel(even_ref, band_ref, own_ref, near_ref, far_ref, read_ref):
    planes, cells, width = own_ref.shape
    heights = read_ref.shape[0]
    depth = band_ref.shape[1]
    window = 2 * cells + SUB
    even = even_ref[0] == 1
    near, far = near_ref[...], far_ref[...]
    before = jnp.where(even, far, near)
    after = jnp.where(even, near, far)
    scales = [[] for _ in range(heights)]
    for b in range(0, cells // SUB, 2):
        spans = []
        for at in (b * SUB, (b + 1) * SUB):
            pieces = []
            for c in range(planes):
                pieces += [before[c, at:, :], own_ref[c], after[c, : at + SUB, :]]
            pieces.append(jnp.zeros((depth - planes * window, width), jnp.bfloat16))
            spans.append(jnp.concatenate(pieces, axis=0))
        part = jnp.dot(band_ref[...], jnp.concatenate(spans, axis=1), preferred_element_type=jnp.float32)
        for h in range(heights):
            for k in range(2):
                code, scale = coded(part[h * SUB : (h + 1) * SUB, k * width : (k + 1) * width])
                read_ref[h, pl.ds((b + k) * SUB, SUB), :] = code
                scales[h].append(scale)
    for h in range(heights):
        rest = jnp.ones((read_ref.shape[1] - cells - len(scales[h]), width), jnp.float32)
        read_ref[h, pl.ds(cells, read_ref.shape[1] - cells), :] = jnp.concatenate(scales[h] + [rest], axis=0).astype(jnp.bfloat16)


def span_kernel(gains_ref, read_ref, velocity_ref):
    blocks, height, width = read_ref.shape
    rows = velocity_ref.shape[1]
    cells = height - NOTES
    at = pl.multiple_of(pl.program_id(0) * rows, rows)
    index = lax.broadcasted_iota(jnp.int32, (NOTES, width), 0)
    parts = []
    for j in (ORDER.index(block) for block in range(blocks)):
        notes = read_ref[j, pl.ds(cells, NOTES), :].astype(jnp.float32)
        pieces = []
        for k in range(rows // SUB):
            chosen = index == pl.program_id(0) * (rows // SUB) + k
            scale = jnp.sum(jnp.where(chosen, notes, 0.0), axis=0, keepdims=True)
            pieces.append(decoded(read_ref[j, pl.ds(at + k * SUB, SUB), :], scale))
        parts.append(jnp.concatenate(pieces, axis=0))
    read = jnp.concatenate(parts, axis=1)
    shape = (rows, read.shape[1])
    shifted = [pltpu.roll(read, 1, 1), read, pltpu.roll(read, shape[1] - 1, 1)]
    total = 0.0
    for k in range(3):
        third = 0.0
        for e in range(3):
            third = third + jnp.broadcast_to(gains_ref[3 * k + e, 0:1, 0:1], shape) * shifted[e]
        total = total + (third if k == 1 else pltpu.roll(third, (3 - 3 * k) % shape[1], 1))
    velocity_ref[0] = total


def tap_groups(count, groups):
    step = count // 2
    return [[(g if h < groups // 2 else g ^ step) * groups + h for h in TAP_ORDER] for g in range(count)]


def tied(value, *after):
    return lax.optimization_barrier((value, *after))[0]


def local(wall_history, kernel_taps, span_gains):
    snaps, chans, cells, width = wall_history.shape
    taps = kernel_taps.shape[-1]
    planes = snaps * chans
    window = taps - 1 + SUB
    groups = lax.axis_size("ha")
    count = lax.axis_size("gx")
    depth = -(-planes * window // 128) * 128
    vmem, smem = pl.BlockSpec(memory_space=pltpu.VMEM), pl.BlockSpec(memory_space=pltpu.SMEM)
    params = pltpu.CompilerParams(vmem_limit_bytes=32 * 1024 * 1024)
    long = pl.CostEstimate(flops=40_000_000_000, bytes_accessed=1 << 16, transcendentals=0)

    rows = jnp.broadcast_to(kernel_taps, (groups, snaps, chans, taps))
    own = tied(wall_history.reshape(planes, cells, width), rows)
    rows = lax.all_to_all(rows, ("gx", "ha"), 0, 0, tiled=True, axis_index_groups=tap_groups(count, groups))
    far = lax.ppermute(own, "gx", [(i, (i - 1 if i % 2 == 0 else i + 1) % count) for i in range(count)])
    near = lax.ppermute(own, "gx", [(i, i ^ 1) for i in range(count)])
    wide = pl.pallas_call(
        gains_kernel,
        out_shape=jax.ShapeDtypeStruct((span_gains.shape[1], 8, 128), jnp.float32),
        in_specs=[vmem],
        out_specs=vmem,
        compiler_params=params,
        cost_estimate=long,
    )(span_gains)
    band = pl.pallas_call(
        band_kernel,
        out_shape=jax.ShapeDtypeStruct((groups * SUB, depth), jnp.bfloat16),
        in_specs=[vmem],
        out_specs=vmem,
        compiler_params=params,
    )(tied(rows, wide))
    even = (lax.axis_index("gx") % 2 == 0).astype(jnp.int32).reshape(1)
    read = pl.pallas_call(
        read_kernel,
        out_shape=jax.ShapeDtypeStruct((groups, cells + NOTES, width), jnp.bfloat16),
        in_specs=[smem] + [vmem] * 4,
        out_specs=vmem,
        compiler_params=params,
        cost_estimate=pl.CostEstimate(flops=2 * groups * cells * width * planes * window, bytes_accessed=2 << 20, transcendentals=0),
    )(even, band, own, near, far)
    read = lax.all_to_all(read, "ha", 0, 0, tiled=True, axis_index_groups=[list(ORDER)])
    return pl.pallas_call(
        span_kernel,
        grid=(cells // STEP,),
        out_shape=jax.ShapeDtypeStruct((1, cells, groups * width), jnp.float32),
        in_specs=[vmem, vmem],
        out_specs=pl.BlockSpec((1, STEP, groups * width), lambda i: (0, i, 0)),
        compiler_params=params,
    )(wide, read)


def solution(mesh):
    in_specs = (P(None, None, "gx", "ha"), P("ha", None, None, None), P("ha", None))
    out_specs = P("ha", "gx", None)
    return jax.shard_map(local, mesh=mesh, in_specs=in_specs, out_specs=out_specs, check_vma=False)
```

```python
import jax
import jax.numpy as jnp
from jax import lax
from jax.experimental import pallas as pl
from jax.experimental.pallas import tpu as pltpu
from jax.sharding import PartitionSpec as P

SUB = 16
ORDER = (4, 5, 6, 7, 0, 1, 2, 3)
TAP_ORDER = (6, 7, 5, 4, 2, 3, 1, 0)
NOTES = 16
STEP = 128
LEVELS = 30719.0
OFFSET = 120.0
LOG2E = 1.4426950408889634
TINY = 2.0**-125


def gains_kernel(gains_ref, wide_ref):
    for e in range(gains_ref.shape[1]):
        wide_ref[e] = jnp.broadcast_to(gains_ref[0:1, e : e + 1], wide_ref.shape[1:])


def band_kernel(taps_ref, band_ref):
    heights, snaps, chans, taps = taps_ref.shape
    depth = band_ref.shape[1]
    for h in range(heights):
        pieces = []
        for s in range(snaps):
            for c in range(chans):
                pieces += [taps_ref[h, s, c : c + 1, :].astype(jnp.float32), jnp.zeros((1, SUB - 1), jnp.float32)]
        pieces.append(jnp.zeros((1, depth - snaps * chans * (taps + SUB - 1)), jnp.float32))
        row = jnp.broadcast_to(jnp.concatenate(pieces, axis=1), (SUB, depth))
        band_ref[pl.ds(ORDER.index(TAP_ORDER[h]) * SUB, SUB), :] = pltpu.roll(row, 0, 1, stride=1, stride_axis=0).astype(jnp.bfloat16)


def coded(values):
    peak = jnp.max(jnp.abs(values), axis=0, keepdims=True) * (1 + 1 / 128)
    scale = jnp.maximum(peak.astype(jnp.bfloat16).astype(jnp.float32), TINY)
    level = jnp.floor(jnp.abs(values) * (1.0 / scale) * LEVELS + 0.5) * (1 / 128)
    octave = jnp.floor(level)
    size = (level - octave + 1.0) * jnp.exp2(octave - OFFSET)
    return jnp.where(values < 0, -size, size).astype(jnp.bfloat16), scale


def decoded(code, scale):
    code = code.astype(jnp.float32)
    size = jnp.abs(code)
    octave = jnp.floor(jnp.log(size) * LOG2E)
    level = (octave + (OFFSET - 1.0) + size * jnp.exp2(-octave)) * (scale * (128 / LEVELS))
    return jnp.where(code < 0, -level, level)


def read_kernel(even_ref, band_ref, own_ref, near_ref, far_ref, read_ref):
    planes, cells, width = own_ref.shape
    heights = read_ref.shape[0]
    depth = band_ref.shape[1]
    window = 2 * cells + SUB
    even = even_ref[0] == 1
    near, far = near_ref[...], far_ref[...]
    before = jnp.where(even, far, near)
    after = jnp.where(even, near, far)
    scales = [[] for _ in range(heights)]
    for b in range(0, cells // SUB, 2):
        spans = []
        for at in (b * SUB, (b + 1) * SUB):
            pieces = []
            for c in range(planes):
                pieces += [before[c, at:, :], own_ref[c], after[c, : at + SUB, :]]
            pieces.append(jnp.zeros((depth - planes * window, width), jnp.bfloat16))
            spans.append(jnp.concatenate(pieces, axis=0))
        part = jnp.dot(band_ref[...], jnp.concatenate(spans, axis=1), preferred_element_type=jnp.float32)
        for h in range(heights):
            for k in range(2):
                code, scale = coded(part[h * SUB : (h + 1) * SUB, k * width : (k + 1) * width])
                read_ref[h, pl.ds((b + k) * SUB, SUB), :] = code
                scales[h].append(scale)
    for h in range(heights):
        rest = jnp.ones((read_ref.shape[1] - cells - len(scales[h]), width), jnp.float32)
        read_ref[h, pl.ds(cells, read_ref.shape[1] - cells), :] = jnp.concatenate(scales[h] + [rest], axis=0).astype(jnp.bfloat16)


def span_kernel(gains_ref, read_ref, velocity_ref):
    blocks, height, width = read_ref.shape
    rows = velocity_ref.shape[1]
    cells = height - NOTES
    parts = []
    for j in (ORDER.index(block) for block in range(blocks)):
        notes = read_ref[j, pl.ds(cells, NOTES), :].astype(jnp.float32)
        pieces = []
        for k in range(rows // SUB):
            scale = notes[k : k + 1]
            pieces.append(decoded(read_ref[j, pl.ds(k * SUB, SUB), :], scale))
        parts.append(jnp.concatenate(pieces, axis=0))
    read = jnp.concatenate(parts, axis=1)
    shape = (rows, read.shape[1])
    shifted = [pltpu.roll(read, 1, 1), read, pltpu.roll(read, shape[1] - 1, 1)]
    total = 0.0
    for k in range(3):
        third = 0.0
        for e in range(3):
            third = third + jnp.broadcast_to(gains_ref[3 * k + e, 0:1, 0:1], shape) * shifted[e]
        total = total + (third if k == 1 else pltpu.roll(third, (3 - 3 * k) % shape[1], 1))
    velocity_ref[0] = total


def tap_groups(count, groups):
    step = count // 2
    return [[(g if h < groups // 2 else g ^ step) * groups + h for h in TAP_ORDER] for g in range(count)]


def tied(value, *after):
    return lax.optimization_barrier((value, *after))[0]


def local(wall_history, kernel_taps, span_gains):
    snaps, chans, cells, width = wall_history.shape
    taps = kernel_taps.shape[-1]
    planes = snaps * chans
    window = taps - 1 + SUB
    groups = lax.axis_size("ha")
    count = lax.axis_size("gx")
    depth = -(-planes * window // 128) * 128
    vmem, smem = pl.BlockSpec(memory_space=pltpu.VMEM), pl.BlockSpec(memory_space=pltpu.SMEM)
    params = pltpu.CompilerParams(vmem_limit_bytes=32 * 1024 * 1024)
    long = pl.CostEstimate(flops=40_000_000_000, bytes_accessed=1 << 16, transcendentals=0)

    rows = jnp.broadcast_to(kernel_taps, (groups, snaps, chans, taps))
    own = tied(wall_history.reshape(planes, cells, width), rows)
    rows = lax.all_to_all(rows, ("gx", "ha"), 0, 0, tiled=True, axis_index_groups=tap_groups(count, groups))
    far = lax.ppermute(own, "gx", [(i, (i - 1 if i % 2 == 0 else i + 1) % count) for i in range(count)])
    near = lax.ppermute(own, "gx", [(i, i ^ 1) for i in range(count)])
    wide = pl.pallas_call(
        gains_kernel,
        out_shape=jax.ShapeDtypeStruct((span_gains.shape[1], 8, 128), jnp.float32),
        in_specs=[vmem],
        out_specs=vmem,
        compiler_params=params,
        cost_estimate=long,
    )(span_gains)
    band = pl.pallas_call(
        band_kernel,
        out_shape=jax.ShapeDtypeStruct((groups * SUB, depth), jnp.bfloat16),
        in_specs=[vmem],
        out_specs=vmem,
        compiler_params=params,
    )(tied(rows, wide))
    even = (lax.axis_index("gx") % 2 == 0).astype(jnp.int32).reshape(1)
    read = pl.pallas_call(
        read_kernel,
        out_shape=jax.ShapeDtypeStruct((groups, cells + NOTES, width), jnp.bfloat16),
        in_specs=[smem] + [vmem] * 4,
        out_specs=vmem,
        compiler_params=params,
        cost_estimate=pl.CostEstimate(flops=2 * groups * cells * width * planes * window, bytes_accessed=2 << 20, transcendentals=0),
    )(even, band, own, near, far)
    read = lax.all_to_all(read, "ha", 0, 0, tiled=True, axis_index_groups=[list(ORDER)])
    return pl.pallas_call(
        span_kernel,
        grid=(cells // STEP,),
        out_shape=jax.ShapeDtypeStruct((1, cells, groups * width), jnp.float32),
        in_specs=[vmem, vmem],
        out_specs=pl.BlockSpec((1, STEP, groups * width), lambda i: (0, i, 0)),
        compiler_params=params,
    )(wide, read)


def solution(mesh):
    in_specs = (P(None, None, "gx", "ha"), P("ha", None, None, None), P("ha", None))
    out_specs = P("ha", "gx", None)
    return jax.shard_map(local, mesh=mesh, in_specs=in_specs, out_specs=out_specs, check_vma=False)
```
